768 devices in a mesh: seq: 16 (over y, core), fsdp: 48 (over z, x).
Axes of the slice: x: 4, y: 8, z: 12, core: 2. Of those that a mesh axis runs over, the one named last changes fastest.
Arguments:
- sel_inputs: bfloat16 [48, 1024, 4096], P('fsdp', 'seq'), may hold values from -6 to 6
- val_grads: bfloat16 [48, 1024, 1024], P('fsdp', 'seq'), may hold values from -6 to 6
- positions: int32 [48, 512], P('fsdp'), may hold values from 0 to 4095, as said below
- value_weight: bfloat16 [4096, 1024], P('seq'), may hold values from -0.1875 to 0.1875
- norm_gain: float32 [4096], P('seq'), may hold values from 0.25 to 1.75
Outputs:
- input_grad: bfloat16 [48, 1024, 4096], P('fsdp', 'seq')
- weight_grad: float32 [4096, 1024], P('seq')
- gain_grad: float32 [4096], P('seq')
The draws below stay inside these ranges and needn't reach their ends.
Inputs may be any that keep to these rules, and one draw needn't show every extreme that they name: Each sequence's positions are distinct and increasing; the number that falls in each device's 256 positions is a multiple of 4 and at most 64, and some device of every sequence holds exactly 64.
All inputs are finite; a program needn't handle non-finite values.
Results may differ from the reference program's by a relative error of at most 0.003.
Values may be sent and summed in bfloat16 or wider, within the bound.
No kernel may reach another device: no remote copies, remote signals or barrier semaphores. Data moves between devices by JAX's collectives and lax.ppermute only.
A program may use at most 32 MiB of HBM per device.

```python
import jax
import jax.numpy as jnp
from jax import lax

D = 4096
KVW = 1024
TOK_DEV = 256
ROWS = 64
SELECTED = 512
N_SEQ = 16
N_FSDP = 48


def draw_positions(key, part):
    key = jax.random.fold_in(key, 11)
    half = N_SEQ // 2
    block = TOK_DEV // (4 * N_SEQ)

    def one(seq_key):
        key_a, key_b, key_c = jax.random.split(seq_key, 3)
        order = jax.random.permutation(key_a, N_SEQ)
        shifts = jax.random.randint(key_b, (half,), 0, half + 1).at[0].set(half)
        blocks = jnp.zeros((N_SEQ,), jnp.int32)
        blocks = blocks.at[order[0::2]].set(half + shifts).at[order[1::2]].set(half - shifts)
        counts = blocks * block
        device_keys = jax.random.split(key_c, N_SEQ)
        ranks = jax.vmap(lambda k: jnp.argsort(jax.random.permutation(k, TOK_DEV)))(device_keys)
        chosen = ranks < counts[:, None]
        return jnp.nonzero(chosen.reshape(-1), size=SELECTED)[0].astype(jnp.int32)
    return jax.vmap(one)(jax.random.split(key, N_FSDP))


def steps_of(stream_key, extent, cuts, least, top_value):
    gain, own = 1.0, jax.random.fold_in(stream_key, 6)
    for axis_at, blocks in cuts:
        heights = jnp.exp(jax.random.uniform(jax.random.fold_in(own, axis_at), (blocks,), jnp.float32, least / len(cuts), top_value / len(cuts)))
        gain = gain * jnp.repeat(heights, extent[axis_at] // blocks).reshape([-1 if axis == axis_at else 1 for axis in range(len(extent))])
    return gain


def scatter_about(key, dims, deviation, limit, cuts=(), kind=jnp.bfloat16):
    gain = steps_of(key, dims, cuts, -0.22, 0.18) if cuts else 1.0
    drawn = jax.random.normal(key, dims, jnp.float32) * deviation * gain
    return jnp.minimum(jnp.maximum(drawn, -limit), limit).astype(kind)


def setup_inputs(seed: int = 0) -> dict:
    arg_keys = jax.random.split(jax.random.key(seed), 6)
    sel_inputs = scatter_about(arg_keys[0], (N_FSDP, N_SEQ * ROWS, D), 1.0, 6.0, ((0, 48), (1, 16)))
    val_grads = scatter_about(arg_keys[1], (N_FSDP, N_SEQ * ROWS, KVW), 1.0, 6.0, ((0, 48), (1, 16)))
    positions = draw_positions(jax.random.fold_in(arg_keys[5], 71), 0)
    value_weight = scatter_about(arg_keys[3], (D, KVW), KVW ** -0.5, 0.1875, ((0, 16),))
    norm_gain = jnp.clip(1.0 + 0.15 * jax.random.normal(arg_keys[4], (D,), jnp.float32), 0.25, 1.75)
    return dict(sel_inputs=sel_inputs, val_grads=val_grads, positions=positions, value_weight=value_weight, norm_gain=norm_gain)


EPS = 1e-05

def reference(sel_inputs, val_grads, positions, value_weight, norm_gain):
    rows = TOK_DEV // 4
    slot_ids = jnp.arange(N_SEQ * rows, dtype=jnp.int32)
    owner = slot_ids // rows
    local = slot_ids % rows
    devices = jnp.arange(N_SEQ, dtype=jnp.int32)

    def one(carry, item):
        inputs, grads, places = item
        counts = lax.optimization_barrier(jnp.sum(((places // TOK_DEV)[:, None] == devices[None, :]).astype(jnp.int32), axis=0))
        live = (local < counts[owner]).astype(jnp.float32)
        values = inputs.astype(jnp.float32)
        inv = lax.rsqrt(lax.optimization_barrier(jnp.sum(values * values, axis=1)) / D + EPS) * live
        normed = values * inv[:, None]
        scaled = (normed * norm_gain[None, :]).astype(jnp.bfloat16)
        dnormed = jnp.dot(grads, value_weight.T, preferred_element_type=jnp.float32)
        gained = dnormed * norm_gain[None, :]
        mean_term = lax.optimization_barrier(jnp.sum(gained * normed, axis=1)) / D
        result = (inv[:, None] * (gained - normed * mean_term[:, None])).astype(jnp.bfloat16)
        grad_w = jnp.dot(scaled.T, grads, preferred_element_type=jnp.float32)
        grad_g = lax.optimization_barrier(jnp.sum(dnormed * normed, axis=0))
        return ((carry[0] + grad_w, carry[1] + grad_g), result)
    start = (jnp.zeros((D, KVW), jnp.float32), jnp.zeros((D,), jnp.float32))
    (weight_grad, gain_grad), input_grad = lax.scan(one, start, (sel_inputs, val_grads, positions))
    return (input_grad, weight_grad, gain_grad)
```

```python
import jax
import jax.numpy as jnp
from jax import lax
from jax.experimental import pallas as pl
from jax.experimental.pallas import tpu as pltpu
from jax.sharding import Mesh
from jax.sharding import PartitionSpec as P

D = 4096
KVW = 1024
TOK_DEV = 256
ROWS = 64
EPS = 1e-05
LANES = 128
CHIPS = 8
OWN = D // CHIPS // 2
PLANE = ("zl", "x")
DEEP = "zh"
SWAP = ((0, 1), (1, 0))
F32 = jnp.float32
BF16 = jnp.bfloat16
VMEM = pl.BlockSpec(memory_space=pltpu.VMEM)
SMEM = pl.BlockSpec(memory_space=pltpu.SMEM)


def call(kernel, n_scalars, outs, *args, flops=0, limit=24):
    shapes = [jax.ShapeDtypeStruct(shape, dtype) for shape, dtype in outs]
    sizes = [a.size * a.dtype.itemsize for a in (*args, *shapes)]
    return pl.pallas_call(
        kernel,
        out_shape=shapes,
        in_specs=[SMEM] * n_scalars + [VMEM] * (len(args) - n_scalars),
        out_specs=[VMEM] * len(shapes),
        compiler_params=pltpu.CompilerParams(vmem_limit_bytes=limit << 20),
        cost_estimate=pl.CostEstimate(flops=flops, bytes_accessed=sum(sizes), transcendentals=0),
    )(*args)


def rounded(value):
    return value.astype(BF16).astype(F32)


def exchange(blocks, axis):
    return lax.all_to_all(blocks, axis, 0, 0, tiled=True)


def spread(block, axis):
    return exchange(jnp.broadcast_to(block[None], (lax.axis_size(axis),) + block.shape), axis)


def prepare_kernel(first_ref, places_ref, x_ref, dv_ref, slices_ref, inv_ref):
    first = first_ref[0]
    places = places_ref[...]
    inside = jnp.where((places >= first) & (places < first + TOK_DEV), 1.0, 0.0)
    count = jnp.sum(inside, axis=1, keepdims=True)
    width = D // CHIPS
    squares = jnp.zeros((ROWS, LANES), F32)
    for j in range(CHIPS):
        block = x_ref[:, j * width:(j + 1) * width]
        slices_ref[j, :, :width] = block
        for k in range(0, width, LANES):
            part = block[:, k:k + LANES].astype(F32)
            squares = squares + part * part
    squares = jnp.sum(squares, axis=1, keepdims=True)
    row = lax.broadcasted_iota(jnp.int32, (ROWS, 1), 0).astype(F32)
    inv = jnp.where(row < count, lax.rsqrt(squares / D + EPS), 0.0)
    inv_ref[...] = jnp.broadcast_to(inv, (ROWS, LANES))
    high = rounded(inv)
    middle = rounded(inv - high)
    low = (inv - high) - middle
    lane = lax.broadcasted_iota(jnp.int32, (ROWS, LANES), 1)
    last = dv_ref[:, KVW - 1:].astype(F32)
    extra = jnp.where(lane == 0, last, jnp.where(lane == 1, high, jnp.where(lane == 2, middle, jnp.where(lane == 3, low, 0.0))))
    extra = extra.astype(BF16)
    for j in range(CHIPS):
        slices_ref[j, :, width:] = extra


def products_kernel(core_ref, columns_ref, dv_ref, mine_w, other_w, mine_g, other_g, back_ref, keep_ref, send_ref):
    core = core_ref[0]
    width = D // CHIPS
    extra = columns_ref[:, :, width:].reshape(CHIPS * ROWS, LANES).astype(F32)
    inv = extra[:, 1:2] + extra[:, 2:3] + extra[:, 3:4]
    dv = dv_ref[...]
    for half, w_ref, g_ref, out_ref in ((1 - core, other_w, other_g, send_ref), (core, mine_w, mine_g, keep_ref)):
        at = pl.multiple_of(half * OWN, OWN)
        dnormed = lax.dot_general(dv, w_ref[...], (((1,), (1,)), ((), ())), preferred_element_type=F32)
        gain = g_ref[...]
        back_ref[:, :, pl.ds(at, OWN)] = (dnormed * gain).reshape(CHIPS, ROWS, OWN)
        normed = columns_ref[:, :, pl.ds(at, OWN)].reshape(CHIPS * ROWS, OWN).astype(F32) * inv
        scaled = (normed * gain).astype(BF16)
        out_ref[:OWN, :] = lax.dot_general(scaled, dv, (((0,), (0,)), ((), ())), preferred_element_type=F32)
        out_ref[OWN:, :] = jnp.zeros((8, KVW), F32)
        out_ref[OWN:OWN + 1, :OWN] = jnp.sum(dnormed * normed, axis=0, keepdims=True)


def blocks_kernel(keep_ref, theirs_ref, blocks_ref):
    gain = keep_ref[OWN:OWN + 1, :OWN] + theirs_ref[OWN:OWN + 1, :OWN]
    row = lax.broadcasted_iota(jnp.int32, (16, LANES), 0)
    high = rounded(gain)
    rest = gain - high
    extra = jnp.zeros((16, LANES), F32)
    for i, part in enumerate((high[:, :LANES], high[:, LANES:], rest[:, :LANES], rest[:, LANES:])):
        extra = jnp.where(row == i, part, extra)
    extra = extra.astype(BF16)
    for j in range(16):
        rows = slice(j * 16, (j + 1) * 16)
        blocks_ref[j, :, :KVW] = (keep_ref[rows, :] + theirs_ref[rows, :]).astype(BF16)
        blocks_ref[j, :, KVW:] = extra


def finish_kernel(whole_ref, w_ref, g_ref):
    for j in range(16):
        w_ref[j * 16:(j + 1) * 16, :] = whole_ref[j, :, :KVW].astype(F32)
    extra = whole_ref[0, :, KVW:].astype(F32)
    g_ref[...] = extra[0:2] + extra[2:4]


def rows_kernel(me_ref, x_ref, inv_ref, *refs):
    blocks, out_ref = refs[:-1], refs[-1]
    width = D // CHIPS
    me = me_ref[0]
    spots = [pl.multiple_of(lax.rem(me + CHIPS - k, CHIPS) * width, width) for k in range(CHIPS)]
    total = jnp.zeros((ROWS, LANES), F32)
    for at, block in zip(spots, blocks):
        product = block[...] * x_ref[:, pl.ds(at, width)].astype(F32)
        for k in range(0, width, LANES):
            total = total + product[:, k:k + LANES]
    inv = inv_ref[:, :1]
    mean = inv * (jnp.sum(total, axis=1, keepdims=True) / D)
    shift = inv * mean
    for at, block in zip(spots, blocks):
        values = x_ref[:, pl.ds(at, width)].astype(F32)
        out_ref[:, pl.ds(at, width)] = (inv * (block[...] - values * shift)).astype(BF16)


def sum_gain(part):
    row = lax.broadcasted_iota(jnp.int32, part.shape, 0)
    lane = lax.broadcasted_iota(jnp.int32, part.shape, 1)
    both = part + jnp.concatenate([part[2:], part[:2]])
    return jnp.where((lane >= KVW) & (row < 2), both, part)


def split_gain(part):
    row = lax.broadcasted_iota(jnp.int32, part.shape, 0)
    lane = lax.broadcasted_iota(jnp.int32, part.shape, 1)
    rest = part - lax.reduce_precision(part, 8, 7)
    rest = jnp.concatenate([rest[-2:], rest[:-2]])
    part = jnp.where((lane >= KVW) & (row >= 2) & (row < 4), rest, part)
    return part.astype(BF16)


def body(sel_inputs, val_grads, positions, value_weight, norm_gain):
    inputs, grads = sel_inputs[0], val_grads[0]
    chip, core = lax.axis_index("y"), lax.axis_index("core")
    first = ((chip * 2 + core) * TOK_DEV).reshape(1)
    width = D // CHIPS
    slices, inv = call(
        prepare_kernel, 1,
        [((CHIPS, ROWS, width + LANES), BF16), ((ROWS, LANES), F32)],
        first, positions, inputs, grads,
    )
    columns = exchange(slices, "y")
    other_weight = lax.ppermute(value_weight, "core", SWAP)
    gain = norm_gain.reshape(1, OWN)
    other_gain = lax.ppermute(gain, "core", SWAP)
    most = lax.all_gather(grads[:, :KVW - 1], "y", axis=0, tiled=True)
    last = columns[:, :, width:width + 1].reshape(CHIPS * ROWS, 1)
    grads_all = jnp.concatenate([most, last], axis=1)

    back, keep, send = call(
        products_kernel, 1,
        [((CHIPS, ROWS, width), F32), ((OWN + 8, KVW), F32), ((OWN + 8, KVW), F32)],
        core.reshape(1), columns, grads_all, value_weight, other_weight, gain, other_gain,
        flops=4 * CHIPS * ROWS * width * KVW,
    )
    theirs = lax.ppermute(send, "core", SWAP)
    (blocks,) = call(blocks_kernel, 0, [((16, 16, KVW + LANES), BF16)], keep, theirs)
    part = sum_gain(jnp.sum(exchange(blocks, PLANE).astype(F32), axis=0))

    def moved(k):
        block = lax.dynamic_index_in_dim(back, (chip + k) % CHIPS, 0, keepdims=False)
        if k == 0:
            return block
        return lax.ppermute(block, "y", [(i, (i + k) % CHIPS) for i in range(CHIPS)])

    rows = {k: moved(k) for k in EARLY}
    if EARLY:
        part, rows = lax.optimization_barrier((part, rows))
    one = lax.ppermute(part, DEEP, [(i, (i + 1) % 3) for i in range(3)])
    two = lax.ppermute(part, DEEP, [(i, (i + 2) % 3) for i in range(3)])
    at = lax.axis_index(DEEP)
    zeroth = jnp.where(at == 0, part, jnp.where(at == 1, one, two))
    second = jnp.where(at == 2, part, jnp.where(at == 0, one, two))
    middle = jnp.where(at == 1, part, jnp.where(at == 2, one, two))
    part = split_gain((zeroth + middle) + second)
    whole = spread(part, PLANE)
    rows.update({k: moved(k) for k in range(CHIPS) if k not in EARLY})

    (result,) = call(
        rows_kernel, 1, [((ROWS, D), BF16)],
        chip.reshape(1), inputs, inv, *[rows[k] for k in range(CHIPS)],
    )
    weight_grad, gain_grad = call(
        finish_kernel, 0, [((OWN, KVW), F32), ((2, LANES), F32)], whole
    )
    return result[None], weight_grad, gain_grad.reshape(OWN)


EARLY = (4, 3, 5, 2)


def solution(mesh):
    fine = Mesh(
        mesh.devices.reshape(8, 2, 3, 4, 4), ("y", "core", "zh", "zl", "x")
    )
    seq, fsdp = ("y", "core"), ("zh", "zl", "x")
    return jax.shard_map(
        body,
        mesh=fine,
        in_specs=(P(fsdp, seq, None), P(fsdp, seq, None), P(fsdp, None), P(seq, None), P(seq)),
        out_specs=(P(fsdp, seq, None), P(seq, None), P(seq)),
        check_vma=False,
    )
```

```python
import jax
import jax.numpy as jnp
from jax import lax
from jax.experimental import pallas as pl
from jax.experimental.pallas import tpu as pltpu
from jax.sharding import Mesh
from jax.sharding import PartitionSpec as P

D = 4096
KVW = 1024
TOK_DEV = 256
ROWS = 64
EPS = 1e-05
LANES = 128
CHIPS = 8
OWN = D // CHIPS // 2
SHARES = 8
SHARE = OWN // SHARES
DEPTH = 3
STACK = 6
WIDE = KVW + LANES
PLANE = ("zl", "x")
PAIR = "zm"
DEEP = "zh"
SWAP = ((0, 1), (1, 0))
F32 = jnp.float32
BF16 = jnp.bfloat16
VMEM = pl.BlockSpec(memory_space=pltpu.VMEM)
SMEM = pl.BlockSpec(memory_space=pltpu.SMEM)


def call(kernel, n_scalars, outs, *args, flops=0, limit=24, scratch=(), spaces=None, out_space=pltpu.VMEM):
    shapes = [jax.ShapeDtypeStruct(shape, dtype) for shape, dtype in outs]
    sizes = [a.size * a.dtype.itemsize for a in (*args, *shapes)]
    return pl.pallas_call(
        kernel,
        out_shape=shapes,
        in_specs=[SMEM] * n_scalars + ([pl.BlockSpec(memory_space=space) for space in spaces] if spaces else [VMEM] * (len(args) - n_scalars)),
        out_specs=[pl.BlockSpec(memory_space=out_space)] * len(shapes),
        scratch_shapes=scratch,
        compiler_params=pltpu.CompilerParams(vmem_limit_bytes=int(limit * 2**20)),
        cost_estimate=pl.CostEstimate(flops=flops, bytes_accessed=sum(sizes), transcendentals=0),
    )(*args)


def rounded(value):
    return value.astype(BF16).astype(F32)


def exchange(blocks, axis):
    return lax.all_to_all(blocks, axis, 0, 0, tiled=True)


def prepare_kernel(first_ref, places_in, x_in, dv_in, slices_ref, inv_ref, places_ref, x_ref, dv_ref, arrived):
    copies = [
        pltpu.make_async_copy(x_in, x_ref, arrived.at[0]),
        pltpu.make_async_copy(dv_in, dv_ref, arrived.at[1]),
        pltpu.make_async_copy(places_in, places_ref, arrived.at[2]),
    ]
    for copy in copies:
        copy.start()
    for copy in copies:
        copy.wait()
    first = first_ref[0]
    places = places_ref[...]
    inside = jnp.where((places >= first) & (places < first + TOK_DEV), 1.0, 0.0)
    count = jnp.sum(inside, axis=1, keepdims=True)
    width = D // CHIPS
    squares = jnp.zeros((ROWS, LANES), F32)
    for j in range(CHIPS):
        block = x_ref[:, j * width:(j + 1) * width]
        slices_ref[j, :, :width] = block
        for k in range(0, width, LANES):
            part = block[:, k:k + LANES].astype(F32)
            squares = squares + part * part
    squares = jnp.sum(squares, axis=1, keepdims=True)
    row = lax.broadcasted_iota(jnp.int32, (ROWS, 1), 0).astype(F32)
    inv = jnp.where(row < count, lax.rsqrt(squares / D + EPS), 0.0)
    inv_ref[...] = jnp.broadcast_to(inv, (ROWS, LANES))
    high = rounded(inv)
    middle = rounded(inv - high)
    low = (inv - high) - middle
    lane = lax.broadcasted_iota(jnp.int32, (ROWS, LANES), 1)
    last = dv_ref[:, KVW - 1:].astype(F32)
    extra = jnp.where(lane == 0, last, jnp.where(lane == 1, high, jnp.where(lane == 2, middle, jnp.where(lane == 3, low, 0.0))))
    extra = extra.astype(BF16)
    for j in range(CHIPS):
        slices_ref[j, :, width:] = extra


def stack_kernel(other_ref, mine_ref, stack_ref, done):
    copies = [
        pltpu.make_async_copy(ref, stack_ref.at[i], done.at[i])
        for i, ref in enumerate((other_ref, mine_ref))
    ]
    for copy in copies:
        copy.start()
    for copy in copies:
        copy.wait()


def gain_lanes(high, rest, *others):
    row = lax.broadcasted_iota(jnp.int32, (SHARE, LANES), 0)
    extra = jnp.zeros((SHARE, LANES), F32)
    parts = (high[:, :LANES], high[:, LANES:], rest[:, :LANES], rest[:, LANES:], *others)
    for i, part in enumerate(parts):
        extra = jnp.where(row == i, part, extra)
    return extra


def gain_of(extra):
    return jnp.concatenate([extra[0:1] + extra[2:3], extra[1:2] + extra[3:4]], axis=1)


def products_kernel(
    core_ref, columns_ref, most_ref, weights_in, mine_g, other_g, back_out, blocks_out,
    weights_ref, dv_ref, back_ref, blocks_ref, arrived, left,
):
    copies = [
        pltpu.make_async_copy(weights_in.at[i], weights_ref.at[i], arrived.at[i]) for i in range(2)
    ]
    for copy in copies:
        copy.start()
    core = core_ref[0]
    width = D // CHIPS
    tail = KVW - LANES
    dv_ref[:, :tail] = most_ref[:, :tail]
    dv_ref[:, tail:KVW - 1] = most_ref[:, tail:]
    extra = columns_ref[:, :, width:].reshape(CHIPS * ROWS, LANES).astype(F32)
    inv = extra[:, 1:2] + extra[:, 2:3] + extra[:, 3:4]
    lane = lax.broadcasted_iota(jnp.int32, (CHIPS * ROWS, LANES), 1)
    ending = jnp.where(lane == LANES - 1, extra[:, 0:1], dv_ref[:, tail:].astype(F32))
    dv_ref[:, tail:] = ending.astype(BF16)
    dv = dv_ref[...]
    gained, largest, leaving = [], 0.0, []
    for i, (half, g_ref) in enumerate(((1 - core, other_g), (core, mine_g))):
        copies[i].wait()
        at = pl.multiple_of(half * OWN, OWN)
        dnormed = lax.dot_general(dv, weights_ref[i], (((1,), (1,)), ((), ())), preferred_element_type=F32)
        gain = g_ref[...]
        gained.append((at, dnormed * gain))
        largest = jnp.maximum(largest, jnp.max(jnp.abs(gained[-1][1]), axis=1, keepdims=True))
        normed = columns_ref[:, :, pl.ds(at, OWN)].reshape(CHIPS * ROWS, OWN).astype(F32) * inv
        scaled = (normed * gain).astype(BF16)
        weight = lax.dot_general(scaled, dv, (((0,), (0,)), ((), ())), preferred_element_type=F32)
        total = jnp.sum(dnormed * normed, axis=0, keepdims=True)
        high = rounded(total)
        mark = gain_lanes(high, total - high).astype(BF16)
        for j in range(SHARES):
            blocks_ref[i, j, :, :KVW] = weight[j * SHARE:(j + 1) * SHARE].astype(BF16)
            blocks_ref[i, j, :, KVW:] = mark
        leaving.append(pltpu.make_async_copy(blocks_ref.at[i], blocks_out.at[half], left.at[i]))
        leaving[-1].start()
    power = jnp.floor(jnp.log2(jnp.maximum(largest, 1e-30)))
    scale = jnp.exp2(-power)
    for at, value in gained:
        back_ref[:, :, pl.ds(at, OWN)] = (value * scale).reshape(CHIPS, ROWS, OWN)
    power = jnp.broadcast_to(power, (CHIPS * ROWS, LANES))
    back_ref[:, :, width:] = power.reshape(CHIPS, ROWS, LANES)
    leaving.append(pltpu.make_async_copy(back_ref, back_out, left.at[2]))
    leaving[-1].start()
    for copy in leaving:
        copy.wait()


def exponent(value):
    largest = jnp.max(jnp.max(jnp.abs(value), axis=1, keepdims=True), axis=0, keepdims=True)
    return jnp.floor(jnp.log2(jnp.maximum(largest, 1e-30)))


def pack(weight, gain, part_ref):
    weight_power, gain_power = exponent(weight), exponent(gain)
    part_ref[:, :KVW] = weight * jnp.exp2(-weight_power)
    gain = gain * jnp.exp2(-gain_power)
    high = rounded(gain)
    wide = [jnp.broadcast_to(power, (1, LANES)) for power in (weight_power, gain_power)]
    part_ref[:, KVW:] = gain_lanes(high, gain - high, *wide)


def unpack(part):
    extra = part[:, KVW:]
    return part[:, :KVW] * jnp.exp2(extra[4:5, :1]), gain_of(extra) * jnp.exp2(extra[5:6, :1])


def partial_kernel(blocks_ref, part_ref):
    total = blocks_ref[0].astype(F32)
    for i in range(1, 2 * SHARES):
        total = total + blocks_ref[i].astype(F32)
    pack(total[:, :KVW], gain_of(total[:, KVW:]), part_ref)


def pair_kernel(mine_ref, theirs_ref, part_ref):
    (weight, gain), (more_weight, more_gain) = unpack(mine_ref[...]), unpack(theirs_ref[...])
    pack(weight + more_weight, gain + more_gain, part_ref)


def total_kernel(me_ref, *refs):
    parts, out_ref, held_ref = refs[:DEPTH], refs[-2], refs[-1]
    me = me_ref[0]
    for k, part in enumerate(parts):
        held_ref[lax.rem(me + DEPTH - k, DEPTH)] = part[...]
    weight, gain = unpack(held_ref[0])
    for i in range(1, DEPTH):
        more_weight, more_gain = unpack(held_ref[i])
        weight, gain = weight + more_weight, gain + more_gain
    weight = weight.astype(BF16)
    high = rounded(gain)
    mark = gain_lanes(high, gain - high).astype(BF16)
    for j in range(SHARES):
        out_ref[j, :, :KVW] = weight
        out_ref[j, :, KVW:] = mark


def finish_kernel(whole_ref, w_ref, g_ref):
    for j in range(SHARES):
        w_ref[j * SHARE:(j + 1) * SHARE, :] = whole_ref[j, :, :KVW].astype(F32)
    g_ref[...] = gain_of(whole_ref[0, :, KVW:].astype(F32))


def rows_kernel(x_ref, inv_ref, back_ref, out_ref):
    width = D // CHIPS
    total = jnp.zeros((ROWS, LANES), F32)
    scales = [jnp.exp2(back_ref[j, :, width:width + 1]) for j in range(CHIPS)]
    for j, scale in enumerate(scales):
        product = back_ref[j, :, :width] * x_ref[:, j * width:(j + 1) * width].astype(F32)
        part = product[:, :LANES]
        for k in range(LANES, width, LANES):
            part = part + product[:, k:k + LANES]
        total = total + part * scale
    inv = inv_ref[:, :1]
    mean = inv * (jnp.sum(total, axis=1, keepdims=True) / D)
    shift = inv * mean
    for j, scale in enumerate(scales):
        at = slice(j * width, (j + 1) * width)
        values = x_ref[:, at].astype(F32)
        out_ref[:, at] = (inv * (back_ref[j, :, :width] * scale - values * shift)).astype(BF16)


def body(sel_inputs, val_grads, positions, value_weight, norm_gain):
    inputs, grads = sel_inputs[0], val_grads[0]
    chip, core = lax.axis_index("y"), lax.axis_index("core")
    first = ((chip * 2 + core) * TOK_DEV).reshape(1)
    width = D // CHIPS
    gain = norm_gain.reshape(1, OWN)
    slices, inv = call(
        prepare_kernel, 1,
        [((CHIPS, ROWS, width + LANES), BF16), ((ROWS, LANES), F32)],
        first, positions, inputs, grads,
        spaces=[pltpu.HBM] * 3, limit=56,
        scratch=[
            pltpu.VMEM(positions.shape, jnp.int32), pltpu.VMEM((ROWS, D), BF16),
            pltpu.VMEM((ROWS, KVW), BF16), pltpu.SemaphoreType.DMA((3,)),
        ],
    )
    columns = exchange(slices, "y")
    other_weight = lax.ppermute(value_weight, "core", SWAP)
    other_gain = lax.ppermute(gain, "core", SWAP)
    (weights,) = call(
        stack_kernel, 0, [((STACK, OWN, KVW), BF16)], other_weight, value_weight,
        spaces=[pltpu.HBM] * 2, out_space=pltpu.HBM, scratch=[pltpu.SemaphoreType.DMA((2,))],
    )
    grads, weights = lax.optimization_barrier((grads, weights))
    most = lax.all_gather(grads[:, :KVW - 1], "y", axis=0, tiled=True)

    back, blocks = call(
        products_kernel, 1,
        [((CHIPS, ROWS, width + LANES), F32), ((2, SHARES, SHARE, WIDE), BF16)],
        core.reshape(1), columns, most, weights, gain, other_gain,
        spaces=[pltpu.VMEM] * 2 + [pltpu.HBM] + [pltpu.VMEM] * 2, out_space=pltpu.HBM, limit=52,
        flops=4 * CHIPS * ROWS * width * KVW,
        scratch=[
            pltpu.VMEM((2, OWN, KVW), BF16), pltpu.VMEM((CHIPS * ROWS, KVW), BF16),
            pltpu.VMEM((CHIPS, ROWS, width + LANES), F32), pltpu.VMEM((2, SHARES, SHARE, WIDE), BF16),
            pltpu.SemaphoreType.DMA((2,)), pltpu.SemaphoreType.DMA((3,)),
        ],
    )
    blocks = exchange(blocks.reshape(2 * SHARES, SHARE, WIDE), ("core", *PLANE))
    (part,) = call(partial_kernel, 0, [((SHARE, WIDE), F32)], blocks)

    part, back = lax.optimization_barrier((part.astype(jnp.float16), back.astype(jnp.float16)))
    back = exchange(back, "y")
    theirs = lax.ppermute(part, PAIR, SWAP)
    (part,) = call(pair_kernel, 0, [((SHARE, WIDE), F32)], part.astype(F32), theirs.astype(F32))
    part = lax.optimization_barrier(part.astype(jnp.float16))
    parts = [part] + [
        lax.ppermute(part, DEEP, [(i, (i + k) % DEPTH) for i in range(DEPTH)])
        for k in range(1, DEPTH)
    ]
    (whole,) = call(
        total_kernel, 1, [((SHARES, SHARE, WIDE), BF16)],
        lax.axis_index(DEEP).reshape(1), *[part.astype(F32) for part in parts],
        scratch=[pltpu.VMEM((DEPTH, SHARE, WIDE), F32)],
    )
    whole, back = lax.optimization_barrier((whole, back))
    whole = exchange(whole, PLANE)

    (result,) = call(rows_kernel, 0, [((ROWS, D), BF16)], inputs, inv, back.astype(F32))
    weight_grad, gain_grad = call(
        finish_kernel, 0, [((OWN, KVW), F32), ((1, OWN), F32)], whole
    )
    return result[None], weight_grad, gain_grad.reshape(OWN)


def solution(mesh):
    fine = Mesh(
        mesh.devices.reshape(8, 2, 3, 2, 2, 4), ("y", "core", "zh", "zm", "zl", "x")
    )
    seq, fsdp = ("y", "core"), ("zh", "zm", "zl", "x")
    return jax.shard_map(
        body,
        mesh=fine,
        in_specs=(P(fsdp, seq, None), P(fsdp, seq, None), P(fsdp, None), P(seq, None), P(seq)),
        out_specs=(P(fsdp, seq, None), P(seq, None), P(seq)),
        check_vma=False,
    )
```

```python
import jax
import jax.numpy as jnp
from jax import lax
from jax.experimental import pallas as pl
from jax.experimental.pallas import tpu as pltpu
from jax.sharding import Mesh
from jax.sharding import PartitionSpec as P

D = 4096
KVW = 1024
TOK_DEV = 256
ROWS = 64
EPS = 1e-05
LANES = 128
CHIPS = 8
OWN = D // CHIPS // 2
SHARES = 8
SHARE = OWN // SHARES
DEPTH = 6
STACK = 6
TALL = 256 + 16
PLANE = ("zl", "x")
DEEP = ("zh", "zm")
SWAP = ((0, 1), (1, 0))
F32 = jnp.float32
BF16 = jnp.bfloat16
VMEM = pl.BlockSpec(memory_space=pltpu.VMEM)
SMEM = pl.BlockSpec(memory_space=pltpu.SMEM)


def call(kernel, n_scalars, outs, *args, flops=0, limit=24, scratch=(), spaces=None, out_space=pltpu.VMEM):
    shapes = [jax.ShapeDtypeStruct(shape, dtype) for shape, dtype in outs]
    sizes = [a.size * a.dtype.itemsize for a in (*args, *shapes)]
    return pl.pallas_call(
        kernel,
        out_shape=shapes,
        in_specs=[SMEM] * n_scalars + ([pl.BlockSpec(memory_space=space) for space in spaces] if spaces else [VMEM] * (len(args) - n_scalars)),
        out_specs=[pl.BlockSpec(memory_space=out_space)] * len(shapes),
        scratch_shapes=scratch,
        compiler_params=pltpu.CompilerParams(vmem_limit_bytes=int(limit * 2**20)),
        cost_estimate=pl.CostEstimate(flops=flops, bytes_accessed=sum(sizes), transcendentals=0),
    )(*args)


def rounded(value):
    return value.astype(BF16).astype(F32)


def exchange(blocks, axis):
    return lax.all_to_all(blocks, axis, 0, 0, tiled=True)


def prepare_kernel(first_ref, places_in, x_in, dv_in, slices_ref, inv_ref, places_ref, x_ref, dv_ref, arrived):
    copies = [
        pltpu.make_async_copy(x_in, x_ref, arrived.at[0]),
        pltpu.make_async_copy(dv_in, dv_ref, arrived.at[1]),
        pltpu.make_async_copy(places_in, places_ref, arrived.at[2]),
    ]
    for copy in copies:
        copy.start()
    for copy in copies:
        copy.wait()
    first = first_ref[0]
    places = places_ref[...]
    inside = jnp.where((places >= first) & (places < first + TOK_DEV), 1.0, 0.0)
    count = jnp.sum(inside, axis=1, keepdims=True)
    width = D // CHIPS
    squares = jnp.zeros((ROWS, LANES), F32)
    for j in range(CHIPS):
        block = x_ref[:, j * width:(j + 1) * width]
        slices_ref[j, :, :width] = block
        for k in range(0, width, LANES):
            part = block[:, k:k + LANES].astype(F32)
            squares = squares + part * part
    squares = jnp.sum(squares, axis=1, keepdims=True)
    row = lax.broadcasted_iota(jnp.int32, (ROWS, 1), 0).astype(F32)
    inv = jnp.where(row < count, lax.rsqrt(squares / D + EPS), 0.0)
    inv_ref[...] = jnp.broadcast_to(inv, (ROWS, LANES))
    high = rounded(inv)
    middle = rounded(inv - high)
    low = (inv - high) - middle
    lane = lax.broadcasted_iota(jnp.int32, (ROWS, LANES), 1)
    last = dv_ref[:, KVW - 1:].astype(F32)
    extra = jnp.where(lane == 0, last, jnp.where(lane == 1, high, jnp.where(lane == 2, middle, jnp.where(lane == 3, low, 0.0))))
    extra = extra.astype(BF16)
    for j in range(CHIPS):
        slices_ref[j, :, width:] = extra


def stack_kernel(other_ref, mine_ref, stack_ref, done):
    copies = [
        pltpu.make_async_copy(ref, stack_ref.at[i], done.at[i])
        for i, ref in enumerate((other_ref, mine_ref))
    ]
    for copy in copies:
        copy.start()
    for copy in copies:
        copy.wait()


def gain_rows(high, rest, *others):
    row = lax.broadcasted_iota(jnp.int32, (16, LANES), 0)
    extra = jnp.zeros((16, LANES), F32)
    parts = (high[:, :LANES], high[:, LANES:], rest[:, :LANES], rest[:, LANES:], *others)
    for i, part in enumerate(parts):
        extra = jnp.where(row == i, part, extra)
    return extra


def gain_of(extra):
    return jnp.concatenate([extra[0:1] + extra[2:3], extra[1:2] + extra[3:4]], axis=1)


def products_kernel(
    core_ref, columns_ref, most_ref, weights_in, mine_g, other_g, back_out, blocks_out,
    weights_ref, dv_ref, back_ref, blocks_ref, arrived, left,
):
    copies = [
        pltpu.make_async_copy(weights_in.at[i], weights_ref.at[i], arrived.at[i]) for i in range(2)
    ]
    for copy in copies:
        copy.start()
    core = core_ref[0]
    width = D // CHIPS
    tail = KVW - LANES
    dv_ref[:, :tail] = most_ref[:, :tail]
    dv_ref[:, tail:KVW - 1] = most_ref[:, tail:]
    extra = columns_ref[:, :, width:].reshape(CHIPS * ROWS, LANES).astype(F32)
    inv = extra[:, 1:2] + extra[:, 2:3] + extra[:, 3:4]
    lane = lax.broadcasted_iota(jnp.int32, (CHIPS * ROWS, LANES), 1)
    ending = jnp.where(lane == LANES - 1, extra[:, 0:1], dv_ref[:, tail:].astype(F32))
    dv_ref[:, tail:] = ending.astype(BF16)
    dv = dv_ref[...]
    gained, largest, leaving = [], 0.0, []
    for i, (half, g_ref) in enumerate(((1 - core, other_g), (core, mine_g))):
        copies[i].wait()
        gain = g_ref[...]
        dnormed = lax.dot_general(dv, weights_ref[i], (((1,), (1,)), ((), ())), preferred_element_type=F32)
        gained.append((pl.multiple_of(half * OWN, OWN), dnormed * gain))
        largest = jnp.maximum(largest, jnp.max(jnp.abs(gained[-1][1]), axis=1, keepdims=True))
        at = gained[-1][0]
        normed = columns_ref[:, :, pl.ds(at, OWN)].reshape(CHIPS * ROWS, OWN).astype(F32) * inv
        scaled = (normed * gain).astype(BF16)
        weight = lax.dot_general(scaled, dv, (((0,), (0,)), ((), ())), preferred_element_type=F32)
        total = jnp.sum(dnormed * normed, axis=0, keepdims=True)
        high = rounded(total)
        mark = gain_rows(high, total - high).astype(BF16)
        for j in range(SHARES):
            rows = weight[j * SHARE:(j + 1) * SHARE].astype(BF16)
            for k in range(KVW // LANES):
                blocks_ref[i, j, k * SHARE:(k + 1) * SHARE, :] = rows[:, k * LANES:(k + 1) * LANES]
            blocks_ref[i, j, 256:, :] = mark
        leaving.append(pltpu.make_async_copy(blocks_ref.at[i], blocks_out.at[half], left.at[i]))
        leaving[-1].start()
    power = jnp.floor(jnp.log2(jnp.maximum(largest, 1e-30)))
    scale = jnp.exp2(-power)
    for at, value in gained:
        back_ref[:, :, pl.ds(at, OWN)] = (value * scale).reshape(CHIPS, ROWS, OWN)
    power = jnp.broadcast_to(power, (CHIPS * ROWS, LANES))
    back_ref[:, :, width:] = power.reshape(CHIPS, ROWS, LANES)
    leaving.append(pltpu.make_async_copy(back_ref, back_out, left.at[2]))
    leaving[-1].start()
    for copy in leaving:
        copy.wait()


def exponent(value):
    largest = jnp.max(jnp.max(jnp.abs(value), axis=1, keepdims=True), axis=0, keepdims=True)
    return jnp.floor(jnp.log2(jnp.maximum(largest, 1e-30)))


def pack(weight, gain, part_ref):
    weight_power, gain_power = exponent(weight), exponent(gain)
    part_ref[:256, :] = weight * jnp.exp2(-weight_power)
    gain = gain * jnp.exp2(-gain_power)
    high = rounded(gain)
    wide = [jnp.broadcast_to(power, (1, LANES)) for power in (weight_power, gain_power)]
    part_ref[256:, :] = gain_rows(high, gain - high, *wide)


def unpack(part):
    extra = part[256:]
    return part[:256] * jnp.exp2(extra[4:5, :1]), gain_of(extra) * jnp.exp2(extra[5:6, :1])


def partial_kernel(blocks_ref, part_ref):
    total = blocks_ref[0].astype(F32)
    for i in range(1, 2 * SHARES):
        total = total + blocks_ref[i].astype(F32)
    pack(total[:256], gain_of(total[256:]), part_ref)


def total_kernel(parts_ref, out_ref):
    weight, gain = unpack(parts_ref[0])
    for i in range(1, DEPTH):
        more_weight, more_gain = unpack(parts_ref[i])
        weight, gain = weight + more_weight, gain + more_gain
    weight = weight.astype(BF16)
    high = rounded(gain)
    mark = gain_rows(high, gain - high).astype(BF16)
    for j in range(SHARES):
        out_ref[j, :256, :] = weight
        out_ref[j, 256:, :] = mark


def finish_kernel(whole_ref, w_ref, g_ref):
    for j in range(SHARES):
        for k in range(KVW // LANES):
            part = whole_ref[j, k * SHARE:(k + 1) * SHARE, :].astype(F32)
            w_ref[j * SHARE:(j + 1) * SHARE, k * LANES:(k + 1) * LANES] = part
    g_ref[...] = gain_of(whole_ref[0, 256:, :].astype(F32))


def rows_kernel(x_ref, inv_ref, back_ref, out_ref):
    width = D // CHIPS
    total = jnp.zeros((ROWS, LANES), F32)
    scales = [jnp.exp2(back_ref[j, :, width:width + 1]) for j in range(CHIPS)]
    for j, scale in enumerate(scales):
        product = back_ref[j, :, :width] * x_ref[:, j * width:(j + 1) * width].astype(F32)
        part = product[:, :LANES]
        for k in range(LANES, width, LANES):
            part = part + product[:, k:k + LANES]
        total = total + part * scale
    inv = inv_ref[:, :1]
    mean = inv * (jnp.sum(total, axis=1, keepdims=True) / D)
    shift = inv * mean
    for j, scale in enumerate(scales):
        at = slice(j * width, (j + 1) * width)
        values = x_ref[:, at].astype(F32)
        out_ref[:, at] = (inv * (back_ref[j, :, :width] * scale - values * shift)).astype(BF16)


def body(sel_inputs, val_grads, positions, value_weight, norm_gain):
    inputs, grads = sel_inputs[0], val_grads[0]
    chip, core = lax.axis_index("y"), lax.axis_index("core")
    first = ((chip * 2 + core) * TOK_DEV).reshape(1)
    width = D // CHIPS
    gain = norm_gain.reshape(1, OWN)
    slices, inv = call(
        prepare_kernel, 1,
        [((CHIPS, ROWS, width + LANES), BF16), ((ROWS, LANES), F32)],
        first, positions, inputs, grads,
        spaces=[pltpu.HBM] * 3, limit=56,
        scratch=[
            pltpu.VMEM(positions.shape, jnp.int32), pltpu.VMEM((ROWS, D), BF16),
            pltpu.VMEM((ROWS, KVW), BF16), pltpu.SemaphoreType.DMA((3,)),
        ],
    )
    slices, value_weight, gain = lax.optimization_barrier((slices, value_weight, gain))
    columns = exchange(slices, "y")
    other_weight = lax.ppermute(value_weight, "core", SWAP)
    other_gain = lax.ppermute(gain, "core", SWAP)
    (weights,) = call(
        stack_kernel, 0, [((STACK, OWN, KVW), BF16)], other_weight, value_weight,
        spaces=[pltpu.HBM] * 2, out_space=pltpu.HBM, scratch=[pltpu.SemaphoreType.DMA((2,))],
    )
    grads, weights = lax.optimization_barrier((grads, weights))
    most = lax.all_gather(grads[:, :KVW - 1], "y", axis=0, tiled=True)

    back, blocks = call(
        products_kernel, 1,
        [((CHIPS, ROWS, width + LANES), F32), ((2, SHARES, TALL, LANES), BF16)],
        core.reshape(1), columns, most, weights, gain, other_gain,
        spaces=[pltpu.VMEM] * 2 + [pltpu.HBM] + [pltpu.VMEM] * 2, out_space=pltpu.HBM, limit=52,
        flops=4 * CHIPS * ROWS * width * KVW,
        scratch=[
            pltpu.VMEM((2, OWN, KVW), BF16), pltpu.VMEM((CHIPS * ROWS, KVW), BF16),
            pltpu.VMEM((CHIPS, ROWS, width + LANES), F32), pltpu.VMEM((2, SHARES, TALL, LANES), BF16),
            pltpu.SemaphoreType.DMA((2,)), pltpu.SemaphoreType.DMA((3,)),
        ],
    )
    blocks = exchange(blocks.reshape(2 * SHARES, TALL, LANES), ("core", *PLANE))
    (part,) = call(partial_kernel, 0, [((TALL, LANES), F32)], blocks)

    part, back = lax.optimization_barrier((part.astype(jnp.float16), back.astype(jnp.float16)))
    back = exchange(back, "y")
    parts = lax.all_gather(part, DEEP, axis=0)
    (whole,) = call(
        total_kernel, 0, [((SHARES, TALL, LANES), BF16)], parts.astype(F32)
    )
    whole, back = lax.optimization_barrier((whole, back))
    whole = exchange(whole, PLANE)

    (result,) = call(rows_kernel, 0, [((ROWS, D), BF16)], inputs, inv, back.astype(F32))
    weight_grad, gain_grad = call(
        finish_kernel, 0, [((OWN, KVW), F32), ((1, OWN), F32)], whole
    )
    return result[None], weight_grad, gain_grad.reshape(OWN)


def solution(mesh):
    fine = Mesh(
        mesh.devices.reshape(8, 2, 3, 2, 2, 4), ("y", "core", "zh", "zm", "zl", "x")
    )
    seq, fsdp = ("y", "core"), ("zh", "zm", "zl", "x")
    return jax.shard_map(
        body,
        mesh=fine,
        in_specs=(P(fsdp, seq, None), P(fsdp, seq, None), P(fsdp, None), P(seq, None), P(seq)),
        out_specs=(P(fsdp, seq, None), P(seq, None), P(seq)),
        check_vma=False,
    )
```

```python
import jax
import jax.numpy as jnp
from jax import lax
from jax.experimental import pallas as pl
from jax.experimental.pallas import tpu as pltpu
from jax.sharding import Mesh
from jax.sharding import PartitionSpec as P

D = 4096
KVW = 1024
TOK_DEV = 256
ROWS = 64
EPS = 1e-05
LANES = 128
CHIPS = 8
OWN = D // CHIPS // 2
SHARES = 8
SHARE = OWN // SHARES
DEPTH = 3
STACK = 16
TALL = 256 + 16
PLANE = ("zl", "x")
PAIR = "zm"
DEEP = "zh"
SWAP = ((0, 1), (1, 0))
F32 = jnp.float32
BF16 = jnp.bfloat16
VMEM = pl.BlockSpec(memory_space=pltpu.VMEM)
SMEM = pl.BlockSpec(memory_space=pltpu.SMEM)


def call(kernel, n_scalars, outs, *args, flops=0, limit=24, scratch=(), spaces=None, out_space=pltpu.VMEM):
    shapes = [jax.ShapeDtypeStruct(shape, dtype) for shape, dtype in outs]
    sizes = [a.size * a.dtype.itemsize for a in (*args, *shapes)]
    return pl.pallas_call(
        kernel,
        out_shape=shapes,
        in_specs=[SMEM] * n_scalars + ([pl.BlockSpec(memory_space=space) for space in spaces] if spaces else [VMEM] * (len(args) - n_scalars)),
        out_specs=[pl.BlockSpec(memory_space=out_space)] * len(shapes),
        scratch_shapes=scratch,
        compiler_params=pltpu.CompilerParams(vmem_limit_bytes=int(limit * 2**20)),
        cost_estimate=pl.CostEstimate(flops=flops, bytes_accessed=sum(sizes), transcendentals=0),
    )(*args)


def rounded(value):
    return value.astype(BF16).astype(F32)


def exchange(blocks, axis):
    return lax.all_to_all(blocks, axis, 0, 0, tiled=True)


def prepare_kernel(first_ref, places_in, x_in, dv_in, slices_ref, inv_ref, places_ref, x_ref, dv_ref, arrived):
    copies = [
        pltpu.make_async_copy(x_in, x_ref, arrived.at[0]),
        pltpu.make_async_copy(dv_in, dv_ref, arrived.at[1]),
        pltpu.make_async_copy(places_in, places_ref, arrived.at[2]),
    ]
    for copy in copies:
        copy.start()
    for copy in copies:
        copy.wait()
    first = first_ref[0]
    places = places_ref[...]
    inside = jnp.where((places >= first) & (places < first + TOK_DEV), 1.0, 0.0)
    count = jnp.sum(inside, axis=1, keepdims=True)
    width = D // CHIPS
    squares = jnp.zeros((ROWS, LANES), F32)
    for j in range(CHIPS):
        block = x_ref[:, j * width:(j + 1) * width]
        slices_ref[j, :, :width] = block
        for k in range(0, width, LANES):
            part = block[:, k:k + LANES].astype(F32)
            squares = squares + part * part
    squares = jnp.sum(squares, axis=1, keepdims=True)
    row = lax.broadcasted_iota(jnp.int32, (ROWS, 1), 0).astype(F32)
    inv = jnp.where(row < count, lax.rsqrt(squares / D + EPS), 0.0)
    inv_ref[...] = jnp.broadcast_to(inv, (ROWS, LANES))
    high = rounded(inv)
    middle = rounded(inv - high)
    low = (inv - high) - middle
    lane = lax.broadcasted_iota(jnp.int32, (ROWS, LANES), 1)
    last = dv_ref[:, KVW - 1:].astype(F32)
    extra = jnp.where(lane == 0, last, jnp.where(lane == 1, high, jnp.where(lane == 2, middle, jnp.where(lane == 3, low, 0.0))))
    extra = extra.astype(BF16)
    for j in range(CHIPS):
        slices_ref[j, :, width:] = extra


def stack_kernel(other_ref, mine_ref, stack_ref, done):
    copies = [
        pltpu.make_async_copy(ref, stack_ref.at[i], done.at[i])
        for i, ref in enumerate((other_ref, mine_ref))
    ]
    for copy in copies:
        copy.start()
    for copy in copies:
        copy.wait()


def gain_rows(high, rest, *others):
    row = lax.broadcasted_iota(jnp.int32, (16, LANES), 0)
    extra = jnp.zeros((16, LANES), F32)
    parts = (high[:, :LANES], high[:, LANES:], rest[:, :LANES], rest[:, LANES:], *others)
    for i, part in enumerate(parts):
        extra = jnp.where(row == i, part, extra)
    return extra


def gain_of(extra):
    return jnp.concatenate([extra[0:1] + extra[2:3], extra[1:2] + extra[3:4]], axis=1)


def half_products(columns_ref, most_ref, dv_ref, weight_ref, copy, gain, at, blocks_ref):
    width = D // CHIPS
    tail = KVW - LANES
    dv_ref[:, :tail] = most_ref[:, :tail]
    dv_ref[:, tail:KVW - 1] = most_ref[:, tail:]
    extra = columns_ref[:, :, width:].reshape(CHIPS * ROWS, LANES).astype(F32)
    inv = extra[:, 1:2] + extra[:, 2:3] + extra[:, 3:4]
    lane = lax.broadcasted_iota(jnp.int32, (CHIPS * ROWS, LANES), 1)
    ending = jnp.where(lane == LANES - 1, extra[:, 0:1], dv_ref[:, tail:].astype(F32))
    dv_ref[:, tail:] = ending.astype(BF16)
    dv = dv_ref[...]
    normed = columns_ref[:, :, pl.ds(at, OWN)].reshape(CHIPS * ROWS, OWN).astype(F32) * inv
    scaled = (normed * gain).astype(BF16)
    weight = lax.dot_general(scaled, dv, (((0,), (0,)), ((), ())), preferred_element_type=F32)
    copy.wait()
    dnormed = lax.dot_general(dv, weight_ref[...], (((1,), (1,)), ((), ())), preferred_element_type=F32)
    total = jnp.sum(dnormed * normed, axis=0, keepdims=True)
    zeros = jnp.zeros((1, OWN), F32)
    mark = gain_rows(total, zeros)
    for j in range(SHARES):
        rows = weight[j * SHARE:(j + 1) * SHARE]
        for k in range(KVW // LANES):
            blocks_ref[j, k * SHARE:(k + 1) * SHARE, :] = rows[:, k * LANES:(k + 1) * LANES]
        blocks_ref[j, 256:, :] = mark
    return dnormed * gain


def theirs_kernel(core_ref, columns_ref, most_ref, weights_in, gain_ref, gained_ref, blocks_ref, weight_ref, dv_ref, arrived):
    copy = pltpu.make_async_copy(weights_in.at[0], weight_ref, arrived.at[0])
    copy.start()
    at = pl.multiple_of((1 - core_ref[0]) * OWN, OWN)
    gained_ref[...] = half_products(columns_ref, most_ref, dv_ref, weight_ref, copy, gain_ref[...], at, blocks_ref)


def mine_kernel(core_ref, columns_ref, most_ref, weights_in, gain_ref, gained_in, back_ref, blocks_ref, weight_ref, dv_ref, gained_ref, arrived):
    copies = [
        pltpu.make_async_copy(weights_in.at[1], weight_ref, arrived.at[0]),
        pltpu.make_async_copy(gained_in, gained_ref, arrived.at[1]),
    ]
    for copy in copies:
        copy.start()
    at = pl.multiple_of(core_ref[0] * OWN, OWN)
    mine = half_products(columns_ref, most_ref, dv_ref, weight_ref, copies[0], gain_ref[...], at, blocks_ref)
    copies[1].wait()
    other = gained_ref[...]
    largest = jnp.max(jnp.maximum(jnp.abs(mine), jnp.abs(other)), axis=1, keepdims=True)
    power = jnp.floor(jnp.log2(jnp.maximum(largest, 1e-30)))
    scale = jnp.exp2(-power)
    back_ref[:, :, :OWN] = (mine * scale).reshape(CHIPS, ROWS, OWN)
    back_ref[:, :, OWN:2 * OWN] = (other * scale).reshape(CHIPS, ROWS, OWN)
    power = jnp.broadcast_to(power, (CHIPS * ROWS, LANES))
    back_ref[:, :, 2 * OWN:] = power.reshape(CHIPS, ROWS, LANES)


def blocks_kernel(keep_ref, theirs_ref, blocks_ref):
    gain = gain_of(keep_ref[0, 256:, :]) + gain_of(theirs_ref[0, 256:, :])
    high = rounded(gain)
    mark = gain_rows(high, gain - high).astype(BF16)
    for j in range(SHARES):
        blocks_ref[j, :256, :] = (keep_ref[j, :256, :] + theirs_ref[j, :256, :]).astype(BF16)
        blocks_ref[j, 256:, :] = mark


def exponent(value):
    largest = jnp.max(jnp.max(jnp.abs(value), axis=1, keepdims=True), axis=0, keepdims=True)
    return jnp.floor(jnp.log2(jnp.maximum(largest, 1e-30)))


def pack(weight, gain, part_ref):
    weight_power, gain_power = exponent(weight), exponent(gain)
    part_ref[:256, :] = weight * jnp.exp2(-weight_power)
    gain = gain * jnp.exp2(-gain_power)
    high = rounded(gain)
    wide = [jnp.broadcast_to(power, (1, LANES)) for power in (weight_power, gain_power)]
    part_ref[256:, :] = gain_rows(high, gain - high, *wide)


def unpack(part):
    extra = part[256:]
    return part[:256] * jnp.exp2(extra[4:5, :1]), gain_of(extra) * jnp.exp2(extra[5:6, :1])


def partial_kernel(blocks_ref, part_ref):
    total = blocks_ref[0].astype(F32)
    for i in range(1, SHARES):
        total = total + blocks_ref[i].astype(F32)
    pack(total[:256], gain_of(total[256:]), part_ref)


def pair_kernel(parts_ref, part_ref):
    (weight, gain), (more_weight, more_gain) = unpack(parts_ref[0]), unpack(parts_ref[1])
    pack(weight + more_weight, gain + more_gain, part_ref)


def total_kernel(parts_ref, out_ref):
    weight, gain = unpack(parts_ref[0])
    for i in range(1, DEPTH):
        more_weight, more_gain = unpack(parts_ref[i])
        weight, gain = weight + more_weight, gain + more_gain
    weight = weight.astype(BF16)
    high = rounded(gain)
    mark = gain_rows(high, gain - high).astype(BF16)
    for j in range(SHARES):
        out_ref[j, :256, :] = weight
        out_ref[j, 256:, :] = mark


def finish_kernel(whole_ref, w_ref, g_ref):
    for j in range(SHARES):
        for k in range(KVW // LANES):
            part = whole_ref[j, k * SHARE:(k + 1) * SHARE, :].astype(F32)
            w_ref[j * SHARE:(j + 1) * SHARE, k * LANES:(k + 1) * LANES] = part
    g_ref[...] = gain_of(whole_ref[0, 256:, :].astype(F32))


def rows_kernel(core_ref, x_ref, inv_ref, back_ref, out_ref):
    core = core_ref[0]
    spots = []
    for j in range(CHIPS):
        scale = jnp.exp2(back_ref[j, :, 2 * OWN:2 * OWN + 1])
        for i, half in enumerate((core, 1 - core)):
            at = pl.multiple_of((2 * j + half) * OWN, OWN)
            spots.append((j, slice(i * OWN, (i + 1) * OWN), pl.ds(at, OWN), scale))
    total = jnp.zeros((ROWS, LANES), F32)
    for j, lanes, at, scale in spots:
        product = back_ref[j, :, lanes] * x_ref[:, at].astype(F32)
        total = total + (product[:, :LANES] + product[:, LANES:]) * scale
    inv = inv_ref[:, :1]
    mean = inv * (jnp.sum(total, axis=1, keepdims=True) / D)
    shift = inv * mean
    for j, lanes, at, scale in spots:
        values = x_ref[:, at].astype(F32)
        out_ref[:, at] = (inv * (back_ref[j, :, lanes] * scale - values * shift)).astype(BF16)


def body(sel_inputs, val_grads, positions, value_weight, norm_gain):
    inputs, grads = sel_inputs[0], val_grads[0]
    chip, core = lax.axis_index("y"), lax.axis_index("core")
    first = ((chip * 2 + core) * TOK_DEV).reshape(1)
    width = D // CHIPS
    gain = norm_gain.reshape(1, OWN)
    slices, inv = call(
        prepare_kernel, 1,
        [((CHIPS, ROWS, width + LANES), BF16), ((ROWS, LANES), F32)],
        first, positions, inputs, grads,
        spaces=[pltpu.HBM] * 3, limit=56,
        scratch=[
            pltpu.VMEM(positions.shape, jnp.int32), pltpu.VMEM((ROWS, D), BF16),
            pltpu.VMEM((ROWS, KVW), BF16), pltpu.SemaphoreType.DMA((3,)),
        ],
    )
    slices, value_weight, gain = lax.optimization_barrier((slices, value_weight, gain))
    columns = exchange(slices, "y")
    other_weight = lax.ppermute(value_weight, "core", SWAP)
    other_gain = lax.ppermute(gain, "core", SWAP)
    (weights,) = call(
        stack_kernel, 0, [((STACK, OWN, KVW), BF16)], other_weight, value_weight,
        spaces=[pltpu.HBM] * 2, out_space=pltpu.HBM, scratch=[pltpu.SemaphoreType.DMA((2,))], limit=50,
    )
    grads, weights = lax.optimization_barrier((grads, weights))
    most = lax.all_gather(grads[:, :KVW - 1], "y", axis=0, tiled=True)

    spaces = [pltpu.VMEM] * 2 + [pltpu.HBM, pltpu.VMEM]
    shape = ((SHARES, TALL, LANES), F32)
    gained, send = call(
        theirs_kernel, 1, [((CHIPS * ROWS, OWN), F32), shape],
        core.reshape(1), columns, most, weights, other_gain,
        spaces=spaces, limit=47, flops=2 * CHIPS * ROWS * width * KVW,
        scratch=[
            pltpu.VMEM((OWN, KVW), BF16), pltpu.VMEM((CHIPS * ROWS, KVW), BF16),
            pltpu.SemaphoreType.DMA((1,)),
        ],
    )
    theirs = lax.ppermute(send, "core", SWAP)
    back, keep = call(
        mine_kernel, 1, [((CHIPS, ROWS, width + LANES), F32), shape],
        core.reshape(1), columns, most, weights, gain, gained,
        spaces=spaces + [pltpu.HBM], limit=47, flops=2 * CHIPS * ROWS * width * KVW,
        scratch=[
            pltpu.VMEM((OWN, KVW), BF16), pltpu.VMEM((CHIPS * ROWS, KVW), BF16),
            pltpu.VMEM((CHIPS * ROWS, OWN), F32), pltpu.SemaphoreType.DMA((2,)),
        ],
    )
    (blocks,) = call(blocks_kernel, 0, [((SHARES, TALL, LANES), BF16)], keep, theirs)
    blocks = exchange(blocks, PLANE)
    (part,) = call(partial_kernel, 0, [((TALL, LANES), F32)], blocks)

    part, back = lax.optimization_barrier((part.astype(jnp.float16), back.astype(jnp.float16)))
    back = exchange(back, "y")
    parts = lax.all_gather(part, PAIR, axis=0)
    (part,) = call(pair_kernel, 0, [((TALL, LANES), F32)], parts.astype(F32))
    parts = lax.all_gather(part.astype(jnp.float16), DEEP, axis=0)
    (whole,) = call(
        total_kernel, 0, [((SHARES, TALL, LANES), BF16)], parts.astype(F32)
    )
    whole, back = lax.optimization_barrier((whole, back))
    whole = exchange(whole, PLANE)

    (result,) = call(
        rows_kernel, 1, [((ROWS, D), BF16)], core.reshape(1), inputs, inv, back.astype(F32)
    )
    weight_grad, gain_grad = call(
        finish_kernel, 0, [((OWN, KVW), F32), ((1, OWN), F32)], whole
    )
    return result[None], weight_grad, gain_grad.reshape(OWN)


def solution(mesh):
    fine = Mesh(
        mesh.devices.reshape(8, 2, 3, 2, 2, 4), ("y", "core", "zh", "zm", "zl", "x")
    )
    seq, fsdp = ("y", "core"), ("zh", "zm", "zl", "x")
    return jax.shard_map(
        body,
        mesh=fine,
        in_specs=(P(fsdp, seq, None), P(fsdp, seq, None), P(fsdp, None), P(seq, None), P(seq)),
        out_specs=(P(fsdp, seq, None), P(seq, None), P(seq)),
        check_vma=False,
    )
```

```python
import jax
import jax.numpy as jnp
from jax import lax
from jax.experimental import pallas as pl
from jax.experimental.pallas import tpu as pltpu
from jax.sharding import Mesh
from jax.sharding import PartitionSpec as P

D = 4096
KVW = 1024
TOK_DEV = 256
ROWS = 64
EPS = 1e-05
LANES = 128
CHIPS = 8
OWN = D // CHIPS // 2
SHARES = 8
SHARE = OWN // SHARES
DEPTH = 3
STACK = 16
TALL = 256 + 16
PLANE = ("zl", "x")
PAIR = "zm"
DEEP = "zh"
SWAP = ((0, 1), (1, 0))
F32 = jnp.float32
BF16 = jnp.bfloat16
VMEM = pl.BlockSpec(memory_space=pltpu.VMEM)
SMEM = pl.BlockSpec(memory_space=pltpu.SMEM)


def call(kernel, n_scalars, outs, *args, flops=0, limit=24, scratch=(), spaces=None, out_space=pltpu.VMEM):
    shapes = [jax.ShapeDtypeStruct(shape, dtype) for shape, dtype in outs]
    sizes = [a.size * a.dtype.itemsize for a in (*args, *shapes)]
    return pl.pallas_call(
        kernel,
        out_shape=shapes,
        in_specs=[SMEM] * n_scalars + ([pl.BlockSpec(memory_space=space) for space in spaces] if spaces else [VMEM] * (len(args) - n_scalars)),
        out_specs=[pl.BlockSpec(memory_space=out_space)] * len(shapes),
        scratch_shapes=scratch,
        compiler_params=pltpu.CompilerParams(vmem_limit_bytes=int(limit * 2**20)),
        cost_estimate=pl.CostEstimate(flops=flops, bytes_accessed=sum(sizes), transcendentals=0),
    )(*args)


def rounded(value):
    return value.astype(BF16).astype(F32)


def exchange(blocks, axis):
    return lax.all_to_all(blocks, axis, 0, 0, tiled=True)


def prepare_kernel(first_ref, places_ref, x_ref, dv_ref, slices_ref, inv_ref):
    first = first_ref[0]
    places = places_ref[...]
    inside = jnp.where((places >= first) & (places < first + TOK_DEV), 1.0, 0.0)
    count = jnp.sum(inside, axis=1, keepdims=True)
    width = D // CHIPS
    squares = jnp.zeros((ROWS, LANES), F32)
    for j in range(CHIPS):
        block = x_ref[:, j * width:(j + 1) * width]
        slices_ref[j, :, :width] = block
        for k in range(0, width, LANES):
            part = block[:, k:k + LANES].astype(F32)
            squares = squares + part * part
    squares = jnp.sum(squares, axis=1, keepdims=True)
    row = lax.broadcasted_iota(jnp.int32, (ROWS, 1), 0).astype(F32)
    inv = jnp.where(row < count, lax.rsqrt(squares / D + EPS), 0.0)
    inv_ref[...] = jnp.broadcast_to(inv, (ROWS, LANES))
    high = rounded(inv)
    middle = rounded(inv - high)
    low = (inv - high) - middle
    lane = lax.broadcasted_iota(jnp.int32, (ROWS, LANES), 1)
    last = dv_ref[:, KVW - 1:].astype(F32)
    extra = jnp.where(lane == 0, last, jnp.where(lane == 1, high, jnp.where(lane == 2, middle, jnp.where(lane == 3, low, 0.0))))
    extra = extra.astype(BF16)
    for j in range(CHIPS):
        slices_ref[j, :, width:] = extra


def stack_kernel(other_ref, mine_ref, stack_ref, done):
    copies = [
        pltpu.make_async_copy(ref, stack_ref.at[i], done.at[i])
        for i, ref in enumerate((other_ref, mine_ref))
    ]
    for copy in copies:
        copy.start()
    for copy in copies:
        copy.wait()


def gain_rows(high, rest, *others):
    row = lax.broadcasted_iota(jnp.int32, (16, LANES), 0)
    extra = jnp.zeros((16, LANES), F32)
    parts = (high[:, :LANES], high[:, LANES:], rest[:, :LANES], rest[:, LANES:], *others)
    for i, part in enumerate(parts):
        extra = jnp.where(row == i, part, extra)
    return extra


def gain_of(extra):
    return jnp.concatenate([extra[0:1] + extra[2:3], extra[1:2] + extra[3:4]], axis=1)


def half_products(columns_ref, most_ref, dv_ref, weight_ref, copy, gain, at, blocks_ref):
    width = D // CHIPS
    tail = KVW - LANES
    dv_ref[:, :tail] = most_ref[:, :tail]
    dv_ref[:, tail:KVW - 1] = most_ref[:, tail:]
    extra = columns_ref[:, :, width:].reshape(CHIPS * ROWS, LANES).astype(F32)
    inv = extra[:, 1:2] + extra[:, 2:3] + extra[:, 3:4]
    lane = lax.broadcasted_iota(jnp.int32, (CHIPS * ROWS, LANES), 1)
    ending = jnp.where(lane == LANES - 1, extra[:, 0:1], dv_ref[:, tail:].astype(F32))
    dv_ref[:, tail:] = ending.astype(BF16)
    dv = dv_ref[...]
    normed = columns_ref[:, :, pl.ds(at, OWN)].reshape(CHIPS * ROWS, OWN).astype(F32) * inv
    scaled = (normed * gain).astype(BF16)
    weight = lax.dot_general(scaled, dv, (((0,), (0,)), ((), ())), preferred_element_type=F32)
    copy.wait()
    dnormed = lax.dot_general(dv, weight_ref[...], (((1,), (1,)), ((), ())), preferred_element_type=F32)
    total = jnp.sum(dnormed * normed, axis=0, keepdims=True)
    zeros = jnp.zeros((1, OWN), F32)
    mark = gain_rows(total, zeros)
    for j in range(SHARES):
        rows = weight[j * SHARE:(j + 1) * SHARE]
        for k in range(KVW // LANES):
            blocks_ref[j, k * SHARE:(k + 1) * SHARE, :] = rows[:, k * LANES:(k + 1) * LANES]
        blocks_ref[j, 256:, :] = mark
    return dnormed * gain


def theirs_kernel(core_ref, columns_ref, most_ref, weights_in, gain_ref, gained_ref, blocks_ref, weight_ref, dv_ref, arrived):
    copy = pltpu.make_async_copy(weights_in.at[0], weight_ref, arrived.at[0])
    copy.start()
    at = pl.multiple_of((1 - core_ref[0]) * OWN, OWN)
    gained_ref[...] = half_products(columns_ref, most_ref, dv_ref, weight_ref, copy, gain_ref[...], at, blocks_ref)


def mine_kernel(core_ref, columns_ref, most_ref, weights_in, gain_ref, gained_in, back_ref, blocks_ref, weight_ref, dv_ref, gained_ref, arrived):
    copies = [
        pltpu.make_async_copy(weights_in.at[1], weight_ref, arrived.at[0]),
        pltpu.make_async_copy(gained_in, gained_ref, arrived.at[1]),
    ]
    for copy in copies:
        copy.start()
    at = pl.multiple_of(core_ref[0] * OWN, OWN)
    mine = half_products(columns_ref, most_ref, dv_ref, weight_ref, copies[0], gain_ref[...], at, blocks_ref)
    copies[1].wait()
    other = gained_ref[...]
    largest = jnp.max(jnp.maximum(jnp.abs(mine), jnp.abs(other)), axis=1, keepdims=True)
    power = jnp.floor(jnp.log2(jnp.maximum(largest, 1e-30)))
    scale = jnp.exp2(-power)
    back_ref[:, :, :OWN] = (mine * scale).reshape(CHIPS, ROWS, OWN)
    back_ref[:, :, OWN:2 * OWN] = (other * scale).reshape(CHIPS, ROWS, OWN)
    power = jnp.broadcast_to(power, (CHIPS * ROWS, LANES))
    back_ref[:, :, 2 * OWN:] = power.reshape(CHIPS, ROWS, LANES)


def blocks_kernel(keep_ref, theirs_ref, blocks_ref):
    gain = gain_of(keep_ref[0, 256:, :]) + gain_of(theirs_ref[0, 256:, :])
    high = rounded(gain)
    mark = gain_rows(high, gain - high).astype(BF16)
    for j in range(SHARES):
        blocks_ref[j, :256, :] = (keep_ref[j, :256, :] + theirs_ref[j, :256, :]).astype(BF16)
        blocks_ref[j, 256:, :] = mark


def exponent(value):
    largest = jnp.max(jnp.max(jnp.abs(value), axis=1, keepdims=True), axis=0, keepdims=True)
    return jnp.floor(jnp.log2(jnp.maximum(largest, 1e-30)))


def pack(weight, gain, part_ref):
    weight_power, gain_power = exponent(weight), exponent(gain)
    part_ref[:256, :] = weight * jnp.exp2(-weight_power)
    gain = gain * jnp.exp2(-gain_power)
    high = rounded(gain)
    wide = [jnp.broadcast_to(power, (1, LANES)) for power in (weight_power, gain_power)]
    part_ref[256:, :] = gain_rows(high, gain - high, *wide)


def unpack(part):
    extra = part[256:]
    return part[:256] * jnp.exp2(extra[4:5, :1]), gain_of(extra) * jnp.exp2(extra[5:6, :1])


def partial_kernel(blocks_ref, part_ref):
    total = blocks_ref[0].astype(F32)
    for i in range(1, SHARES):
        total = total + blocks_ref[i].astype(F32)
    pack(total[:256], gain_of(total[256:]), part_ref)


def pair_kernel(parts_ref, part_ref):
    (weight, gain), (more_weight, more_gain) = unpack(parts_ref[0]), unpack(parts_ref[1])
    pack(weight + more_weight, gain + more_gain, part_ref)


def total_kernel(parts_ref, out_ref):
    weight, gain = unpack(parts_ref[0])
    for i in range(1, DEPTH):
        more_weight, more_gain = unpack(parts_ref[i])
        weight, gain = weight + more_weight, gain + more_gain
    weight = weight.astype(BF16)
    high = rounded(gain)
    mark = gain_rows(high, gain - high).astype(BF16)
    for j in range(SHARES):
        out_ref[j, :256, :] = weight
        out_ref[j, 256:, :] = mark


def finish_kernel(whole_ref, w_ref, g_ref):
    for j in range(SHARES):
        for k in range(KVW // LANES):
            part = whole_ref[j, k * SHARE:(k + 1) * SHARE, :].astype(F32)
            w_ref[j * SHARE:(j + 1) * SHARE, k * LANES:(k + 1) * LANES] = part
    g_ref[...] = gain_of(whole_ref[0, 256:, :].astype(F32))


def rows_kernel(core_ref, x_ref, inv_ref, back_ref, out_ref):
    core = core_ref[0]
    spots = []
    for j in range(CHIPS):
        scale = jnp.exp2(back_ref[j, :, 2 * OWN:2 * OWN + 1])
        for i, half in enumerate((core, 1 - core)):
            at = pl.multiple_of((2 * j + half) * OWN, OWN)
            spots.append((j, slice(i * OWN, (i + 1) * OWN), pl.ds(at, OWN), scale))
    total = jnp.zeros((ROWS, LANES), F32)
    for j, lanes, at, scale in spots:
        product = back_ref[j, :, lanes] * x_ref[:, at].astype(F32)
        total = total + (product[:, :LANES] + product[:, LANES:]) * scale
    inv = inv_ref[:, :1]
    mean = inv * (jnp.sum(total, axis=1, keepdims=True) / D)
    shift = inv * mean
    for j, lanes, at, scale in spots:
        values = x_ref[:, at].astype(F32)
        out_ref[:, at] = (inv * (back_ref[j, :, lanes] * scale - values * shift)).astype(BF16)


def body(sel_inputs, val_grads, positions, value_weight, norm_gain):
    inputs, grads = sel_inputs[0], val_grads[0]
    chip, core = lax.axis_index("y"), lax.axis_index("core")
    first = ((chip * 2 + core) * TOK_DEV).reshape(1)
    width = D // CHIPS
    gain = norm_gain.reshape(1, OWN)
    slices, inv = call(
        prepare_kernel, 1,
        [((CHIPS, ROWS, width + LANES), BF16), ((ROWS, LANES), F32)],
        first, positions, inputs, grads,
        limit=56,
    )
    slices, value_weight, gain = lax.optimization_barrier((slices, value_weight, gain))
    columns = exchange(slices, "y")
    other_weight = lax.ppermute(value_weight, "core", SWAP)
    other_gain = lax.ppermute(gain, "core", SWAP)
    (weights,) = call(
        stack_kernel, 0, [((STACK, OWN, KVW), BF16)], other_weight, value_weight,
        spaces=[pltpu.HBM] * 2, out_space=pltpu.HBM, scratch=[pltpu.SemaphoreType.DMA((2,))], limit=50,
    )
    grads, weights = lax.optimization_barrier((grads, weights))
    most = lax.all_gather(grads[:, :KVW - 1], "y", axis=0, tiled=True)

    spaces = [pltpu.VMEM] * 2 + [pltpu.HBM, pltpu.VMEM]
    shape = ((SHARES, TALL, LANES), F32)
    gained, send = call(
        theirs_kernel, 1, [((CHIPS * ROWS, OWN), F32), shape],
        core.reshape(1), columns, most, weights, other_gain,
        spaces=spaces, limit=47, flops=2 * CHIPS * ROWS * width * KVW,
        scratch=[
            pltpu.VMEM((OWN, KVW), BF16), pltpu.VMEM((CHIPS * ROWS, KVW), BF16),
            pltpu.SemaphoreType.DMA((1,)),
        ],
    )
    theirs = lax.ppermute(send, "core", SWAP)
    back, keep = call(
        mine_kernel, 1, [((CHIPS, ROWS, width + LANES), F32), shape],
        core.reshape(1), columns, most, weights, gain, gained,
        spaces=spaces + [pltpu.HBM], limit=47, flops=2 * CHIPS * ROWS * width * KVW,
        scratch=[
            pltpu.VMEM((OWN, KVW), BF16), pltpu.VMEM((CHIPS * ROWS, KVW), BF16),
            pltpu.VMEM((CHIPS * ROWS, OWN), F32), pltpu.SemaphoreType.DMA((2,)),
        ],
    )
    (blocks,) = call(blocks_kernel, 0, [((SHARES, TALL, LANES), BF16)], keep, theirs)
    blocks = exchange(blocks, PLANE)
    (part,) = call(partial_kernel, 0, [((TALL, LANES), F32)], blocks)

    part, back = lax.optimization_barrier((part.astype(jnp.float16), back.astype(jnp.float16)))
    back = exchange(back, "y")
    parts = lax.all_gather(part, PAIR, axis=0)
    (part,) = call(pair_kernel, 0, [((TALL, LANES), F32)], parts.astype(F32))
    parts = lax.all_gather(part.astype(jnp.float16), DEEP, axis=0)
    (whole,) = call(
        total_kernel, 0, [((SHARES, TALL, LANES), BF16)], parts.astype(F32)
    )
    whole, back = lax.optimization_barrier((whole, back))
    whole = exchange(whole, PLANE)

    (result,) = call(
        rows_kernel, 1, [((ROWS, D), BF16)], core.reshape(1), inputs, inv, back.astype(F32)
    )
    weight_grad, gain_grad = call(
        finish_kernel, 0, [((OWN, KVW), F32), ((1, OWN), F32)], whole
    )
    return result[None], weight_grad, gain_grad.reshape(OWN)


def solution(mesh):
    fine = Mesh(
        mesh.devices.reshape(8, 2, 3, 2, 2, 4), ("y", "core", "zh", "zm", "zl", "x")
    )
    seq, fsdp = ("y", "core"), ("zh", "zm", "zl", "x")
    return jax.shard_map(
        body,
        mesh=fine,
        in_specs=(P(fsdp, seq, None), P(fsdp, seq, None), P(fsdp, None), P(seq, None), P(seq)),
        out_specs=(P(fsdp, seq, None), P(seq, None), P(seq)),
        check_vma=False,
    )
```
